512 devices in a mesh: dp: 4 (over x), trow: 16 (over z_lo, core), tcol: 8 (over y, z_hi).
Axes of the slice: x: 4, y: 4, z: 16 (z_hi: 2, z_lo: 8; z = z_hi * 8 + z_lo), core: 2. Of those that a mesh axis runs over, the one named last changes fastest.
Arguments:
- hidden_in: bfloat16 [2048, 28672], P(('dp', 'tcol'), 'trow'), may hold values from -6 to 6
- down_weight: bfloat16 [28672, 8192], P('trow', 'tcol'), may hold values from -0.03125 to 0.03125
- block_scales: float32 [224, 64], P('trow', 'tcol'), may hold values from 0.5 to 2
- residual: bfloat16 [2048, 8192], P('dp', ('tcol', 'trow')), may hold values from -6 to 6
- projector: bfloat16 [8192, 1536], P(('tcol', 'trow')), may hold values from -0.0625 to 0.0625
- student: bfloat16 [2048, 1536], P(('dp', 'trow', 'tcol')), may hold values from -6 to 6
- segments: int32 [4, 512], P('dp'), may hold values from 0 to 7, never falling along the last dimension, each value on 1 to 192 neighbouring positions
Outputs:
- student_grad: float32 [2048, 1536], P(('dp', 'trow', 'tcol'))
- projector_grad: float32 [8192, 1536], P(('tcol', 'trow'))
The draws below stay inside these ranges and needn't reach their ends.
Inputs may be any that keep to these rules, and one draw needn't show every extreme that they name: `segments`: within each group the passage numbers never fall, every number of 0 to 7 appears, and one passage has exactly 192 tokens.
All inputs are finite; a program needn't handle non-finite values.
Results may differ from the reference program's by a relative error of at most 0.029.
Values may be sent and summed in bfloat16 or wider, within the bound.
No kernel may reach another device: no remote copies, remote signals or barrier semaphores. Data moves between devices by JAX's collectives and lax.ppermute only.
A program may use at most 64 MiB of HBM per device.

```python
import math
import jax
import jax.numpy as jnp
import numpy as np
from jax import lax

D = 8192
FF = 28672
S = 1536
BLOCK = 128
TOK_DEV = 512
COUNT = 8
MOST = 192
GROUPS = 4
TOKENS = 2048
N_TROW = 16


def steps_of(key, extent, pieces, low, top_value):
    factor_of, own = 1.0, jax.random.fold_in(key, 6)
    for axis_at, shards_of in pieces:
        steps = jnp.exp(jax.random.uniform(jax.random.fold_in(own, axis_at), (shards_of,), jnp.float32, low / len(pieces), top_value / len(pieces)))
        factor_of = factor_of * jnp.repeat(steps, extent[axis_at] // shards_of).reshape([-1 if axis == axis_at else 1 for axis in range(len(extent))])
    return factor_of


def split_up(count, total, reach, skew):
    loads = [(1 << 20) // math.isqrt(standing ** skew) + 1 for standing in range(2, count + 1)]
    surplus, counts = total - reach - (count - 1), [1] * (count - 1)
    while surplus > 0:
        movable = [i for i in range(count - 1) if counts[i] < reach]
        mass, left = sum([loads[i] for i in movable]), surplus
        for i in movable:
            extra = min(reach - counts[i], max(1, left * loads[i] // mass), surplus)
            counts[i] = counts[i] + extra
            surplus = surplus - extra
    return np.array([reach] + counts)


def uneven_parts(stream_key, amount, total, most, slope):
    if amount == 2:
        one = jax.random.randint(stream_key, (), max(1, total - most), min(most, total - 1) + 1)
        return jnp.stack([one, total - one])
    sizes = jnp.asarray(split_up(amount, total, most, slope), jnp.int32)
    pairs = (amount - 1) // 2
    giver, taker = sizes[1:1 + 2 * pairs:2], sizes[2:2 + 2 * pairs:2]
    margin = jnp.minimum(giver - 1, most - taker)
    passed = jax.random.randint(jax.random.fold_in(stream_key, 1), (pairs,), 0, 1 << 20) % (margin + 1)
    sizes = sizes.at[1:1 + 2 * pairs:2].set(giver - passed).at[2:2 + 2 * pairs:2].set(taker + passed)
    return sizes[jax.random.permutation(jax.random.fold_in(stream_key, 2), amount)]


def centred(stream_key, extent, deviation, bound, pieces=(), held_as=jnp.bfloat16):
    level = steps_of(stream_key, extent, pieces, -0.22, 0.18) if pieces else 1.0
    drawn = jax.random.normal(stream_key, extent, jnp.float32) * deviation * level
    return jnp.minimum(jnp.maximum(drawn, -bound), bound).astype(held_as)


def setup_inputs(seed: int = 0) -> dict:
    seeds = jax.random.split(jax.random.key(seed), 8)
    hidden_in = centred(seeds[0], (TOKENS, FF), 1.0, 6.0, ((0, 32), (1, 16)))
    down_weight = centred(seeds[1], (FF, D), FF ** -0.5, 0.03125, ((0, 16), (1, 8)))
    block_scales = jnp.clip(jnp.exp(math.log(2.0) - 1.3862944 * jax.random.uniform(seeds[2], (FF // BLOCK, D // BLOCK), jnp.float32) ** steps_of(seeds[2], (FF // BLOCK, D // BLOCK), ((0, 16), (1, 8)), -0.2, 0.2)), 0.5, 2.0)
    residual = centred(seeds[3], (TOKENS, D), 1.0, 6.0, ((0, 4), (1, 128)))
    projector = centred(seeds[4], (D, S), D ** -0.5, 0.0625, ((0, 128),))
    student = centred(seeds[5], (TOKENS, S), 1.0, 6.0, ((0, 512),))
    segments = jax.vmap(lambda own: jnp.searchsorted(jnp.cumsum(uneven_parts(own, COUNT, TOK_DEV, MOST, 1)), jnp.arange(TOK_DEV), side="right"))(jax.random.split(seeds[6], GROUPS)).reshape((GROUPS, TOK_DEV)).astype(jnp.int32)
    return dict(hidden_in=hidden_in, down_weight=down_weight, block_scales=block_scales, residual=residual, projector=projector, student=student, segments=segments)


def reference(hidden_in, down_weight, block_scales, residual, projector, student, segments):
    band = FF // N_TROW

    def step(total, index):
        start = index * band
        weight_band = lax.dynamic_slice_in_dim(down_weight, start, band, 0)
        scale_band = lax.dynamic_slice_in_dim(block_scales, index * (band // BLOCK), band // BLOCK, 0)
        effective = (weight_band.reshape(band // BLOCK, BLOCK, D // BLOCK, BLOCK).astype(jnp.float32) * scale_band[:, None, :, None]).reshape(band, D).astype(jnp.bfloat16)
        rows_band = lax.dynamic_slice_in_dim(hidden_in, start, band, 1)
        part = jnp.dot(rows_band, effective, preferred_element_type=jnp.float32).astype(jnp.bfloat16)
        part = lax.optimization_barrier(part)
        return (total + part.astype(jnp.float32), None)
    teacher, _ = lax.scan(step, jnp.zeros((TOKENS, D), jnp.float32), jnp.arange(N_TROW, dtype=jnp.int32))
    hidden = (residual.astype(jnp.float32) + teacher).astype(jnp.bfloat16)
    projected = jnp.dot(hidden, projector, preferred_element_type=jnp.float32)
    error = projected - student.astype(jnp.float32)
    same = (segments[:, :, None] == segments[:, None, :]).astype(jnp.float32)
    lengths = lax.optimization_barrier(jnp.sum(same, axis=2)).reshape(TOKENS)
    weight = jnp.float32(TOK_DEV) / (COUNT * lengths)
    scaled_f = weight[:, None] * error
    student_grad = -scaled_f
    scaled = scaled_f.astype(jnp.bfloat16)
    grad = lax.dot_general(hidden, scaled, (((0,), (0,)), ((), ())), preferred_element_type=jnp.float32)
    return (student_grad, grad / math.sqrt(TOKENS))
```

```python
import math

import jax
import jax.numpy as jnp
from jax import lax
from jax.sharding import PartitionSpec as P

BLOCK = 128
COUNT = 8
BF = jnp.bfloat16
F32 = jnp.float32


def swap(x, axis, mask):
    return lax.ppermute(x, axis, [(i, i ^ mask) for i in range(lax.axis_size(axis))])


def pick(x, index, axis):
    return lax.dynamic_index_in_dim(x, index, axis, keepdims=False)


def halve(x, axis, mask, bit, at):
    got = swap(pick(x, 1 - bit, at), axis, mask)
    return (pick(x, bit, at).astype(F32) + got.astype(F32)).astype(BF)


def join(x, axis, mask, bit, at):
    got = swap(x, axis, mask)
    return jnp.where(bit == 0, jnp.concatenate([x, got], at), jnp.concatenate([got, x], at))


def shards(hidden_in, down_weight, block_scales, residual, projector, student, segments):
    x, t, c = lax.axis_index("dp"), lax.axis_index("trow"), lax.axis_index("tcol")
    core, zl0, zl1, zl2 = t & 1, (t >> 1) & 1, (t >> 2) & 1, (t >> 3) & 1
    zh, y0, y1 = c & 1, (c >> 1) & 1, (c >> 2) & 1
    rows, cols = down_weight.shape

    far = swap(hidden_in, "tcol", 1)
    near_all = [hidden_in] + [swap(hidden_in, "tcol", 2 * k) for k in (1, 2, 3)]
    far_all = [far] + [swap(far, "tcol", 2 * k) for k in (1, 2, 3)]

    pg = pick(projector.reshape(4, 16, -1), x, 0)[None, None]
    pg = pg.reshape(1, 1, 1, 16, -1)
    pg = join(pg, "trow", 8, zl2, 0)
    zparts = pg
    got = swap(zparts, "trow", 4)
    a, b = jnp.stack([zparts, got], 1), jnp.stack([got, zparts], 1)
    pg = jnp.where(zl1 == 0, a, b).reshape(4, 1, 1, 16, -1)
    got = swap(pg, "trow", 2)
    a, b = jnp.stack([pg, got], 1), jnp.stack([got, pg], 1)
    pg = jnp.where(zl0 == 0, a, b).reshape(8, 1, 1, 16, -1)
    pg = join(pg, "dp", 1, x & 1, 2)
    got = swap(pg, "dp", 2)
    pg = jnp.where((x >> 1) == 0, jnp.concatenate([pg, got], 2), jnp.concatenate([got, pg], 2))
    pg = join(pg, "trow", 1, core, 1)
    pg = pg.reshape(cols, -1)

    effective = (
        (
            down_weight.reshape(rows // BLOCK, BLOCK, cols // BLOCK, BLOCK).astype(F32)
            * block_scales[:, None, :, None]
        )
        .reshape(rows, cols)
        .astype(BF)
    )
    slots = c ^ jnp.array([0, 2, 4, 6, 1, 3, 5, 7], jnp.int32)
    res = jnp.take(residual.reshape(8, 64, 64), slots, axis=0).reshape(512, 64)
    place = (jnp.arange(cols)[None, :] == t * 64 + jnp.arange(64)[:, None]).astype(BF)
    part = jnp.dot(jnp.concatenate(near_all + far_all, 0), effective, preferred_element_type=F32)
    part = (part + jnp.dot(res, place, preferred_element_type=F32)).astype(BF)

    acc = halve(part.reshape(8, 2, 32, cols), "trow", 1, core, 1)
    acc = halve(acc.reshape(2, 4, 32, cols), "trow", 2, zh ^ zl0, 0)
    acc = halve(acc.reshape(2, 2, 32, cols), "trow", 4, y0 ^ zl1, 1)
    hid = halve(acc, "trow", 8, y1 ^ zl2, 0)

    hid_all = jnp.concatenate([hid] + [swap(hid, "dp", k) for k in (1, 2, 3)], 0)

    mine = (jnp.arange(32) // 4 == c)[:, None]
    own_student = jnp.where(mine, jnp.tile(student.astype(F32), (8, 1)), 0.0)
    err = jnp.dot(hid, pg, preferred_element_type=F32) - own_student
    err = err + swap(err.astype(BF), "tcol", 1).astype(F32)
    sent = err.astype(BF)
    err = err + sum(swap(sent, "tcol", 2 * k).astype(F32) for k in (1, 2, 3))

    passage = segments[0]
    same = (passage[:, None] == passage[None, :]).astype(F32)
    weight_all = F32(512) / (COUNT * jnp.sum(same, axis=1))
    weight = lax.dynamic_slice_in_dim(weight_all, t * 32, 32, 0)
    scaled_f = weight[:, None] * err
    student_grad = -lax.dynamic_slice_in_dim(scaled_f, c * 4, 4, 0)
    scaled = scaled_f.astype(BF)

    quarter = lambda k: lax.dynamic_slice_in_dim(scaled, (x ^ k) * 384, 384, 1)
    scaled_all = jnp.concatenate([quarter(0)] + [swap(quarter(k), "dp", k) for k in (1, 2, 3)], 0)
    grad = lax.dot_general(hid_all, scaled_all, (((0,), (0,)), ((), ())), preferred_element_type=F32)
    grad = grad.astype(BF)
    grad = halve(grad.reshape(8, 2, 64, 384), "trow", 1, core, 1)
    grad = halve(grad.reshape(4, 2, 64, 384), "trow", 2, zl0, 1)
    grad = halve(grad.reshape(2, 2, 64, 384), "trow", 4, zl1, 1)
    grad = halve(grad, "trow", 8, zl2, 0)
    pieces = jnp.stack([grad] + [swap(grad, "dp", k) for k in (1, 2, 3)])
    total = jnp.concatenate([pick(pieces, x ^ k, 0) for k in range(4)], 1)
    factor = 1.0 / math.sqrt(512 * lax.axis_size("dp"))
    return (student_grad, total.astype(F32) * factor)


def solution(mesh):
    in_specs = (
        P(("dp", "tcol"), "trow"),
        P("trow", "tcol"),
        P("trow", "tcol"),
        P("dp", ("tcol", "trow")),
        P(("tcol", "trow"), None),
        P(("dp", "trow", "tcol"), None),
        P("dp", None),
    )
    out_specs = (P(("dp", "trow", "tcol"), None), P(("tcol", "trow"), None))
    return jax.shard_map(shards, mesh=mesh, in_specs=in_specs, out_specs=out_specs, check_vma=False)
```

```python
import math

import jax
import jax.numpy as jnp
from jax import lax
from jax.experimental import pallas as pl
from jax.experimental.pallas import tpu as pltpu
from jax.sharding import Mesh
from jax.sharding import PartitionSpec as P

BLOCK = 128
COUNT = 8
BF = jnp.bfloat16
F32 = jnp.float32


def swap(x, axis, mask):
    return lax.ppermute(x, axis, [(i, i ^ mask) for i in range(lax.axis_size(axis))])


def pick(x, index, axis):
    return lax.dynamic_index_in_dim(x, index, axis, keepdims=False)


def exchange(x, axes):
    return lax.all_to_all(x, axes, 0, 0, tiled=True)


def combine_kernel(c_ref, near_ref, near_got_ref, far_ref, far_got_ref, res_ref, out_ref):
    c = c_ref[0]
    for zs, (keep, got) in enumerate(((near_ref, near_got_ref), (far_ref, far_got_ref))):
        for ys in range(4):
            at = c ^ (2 * ys + zs)
            value = keep[ys].astype(F32) + got[ys].astype(F32) + res_ref[at].astype(F32)
            out_ref[at] = value.astype(BF)


def combine(c, near, near_got, far, far_got, res):
    vmem = pl.BlockSpec(memory_space=pltpu.VMEM)
    return pl.pallas_call(
        combine_kernel,
        out_shape=jax.ShapeDtypeStruct(res.shape, BF),
        in_specs=[pl.BlockSpec(memory_space=pltpu.SMEM)] + [vmem] * 5,
        out_specs=vmem,
        compiler_params=pltpu.CompilerParams(vmem_limit_bytes=16 * 1024 * 1024),
        cost_estimate=pl.CostEstimate(flops=10**6, bytes_accessed=4 * 10**6, transcendentals=0),
    )(c.reshape(1), near, near_got, far, far_got, res)


def shards(hidden_in, down_weight, block_scales, residual, projector, student, segments):
    x, zl, core = lax.axis_index("dp"), lax.axis_index("zl"), lax.axis_index("co")
    y, zh = lax.axis_index("y"), lax.axis_index("zh")
    c = 2 * y + zh
    rows, cols = down_weight.shape
    half = cols // 2

    pg = lax.all_gather(projector, "zl", axis=0, tiled=True)

    far = swap(hidden_in, "zh", 1)
    near_all = [hidden_in] + [swap(hidden_in, "y", k) for k in (1, 2, 3)]
    far_all = [far] + [swap(far, "y", k) for k in (1, 2, 3)]

    effective = (
        (
            down_weight.reshape(rows // BLOCK, BLOCK, cols // BLOCK, BLOCK).astype(F32)
            * block_scales[:, None, :, None]
        )
        .reshape(rows, cols)
        .astype(BF)
    )
    k = jnp.arange(cols)
    source = (k % half) // 64 * 128 + jnp.where(k < half, 1 - core, core) * 64 + k % 64
    order = (jnp.arange(cols)[:, None] == source[None, :]).astype(BF)
    effective = jnp.dot(effective, order, preferred_element_type=F32).astype(BF)
    effective = lax.optimization_barrier(effective)
    place = (jnp.arange(half)[None, :] == zl * 64 + jnp.arange(64)[:, None]).astype(BF)
    res = jnp.dot(residual, place, preferred_element_type=F32).astype(BF).reshape(8, 64, half)

    def bands(pieces):
        part = jnp.dot(jnp.concatenate(pieces, 0), effective, preferred_element_type=F32).astype(BF)
        part = part.reshape(4, 64, cols)
        return part[..., half:], swap(part[..., :half], "co", 1)

    near, near_got = bands(near_all)
    far, far_got = bands(far_all)
    acc = combine(c, near, near_got, far, far_got, res)
    hid = jnp.sum(exchange(acc, "zl").astype(F32), 0).astype(BF)
    hid_all = jnp.stack([hid] + [swap(hid, "dp", k) for k in (1, 2, 3)])
    hid_all = jnp.take(hid_all, x ^ jnp.arange(4), axis=0).reshape(256, half)

    mine = (jnp.arange(64) // 4 == core * 8 + c)[:, None]
    own_student = jnp.where(mine, jnp.tile(student.astype(F32), (16, 1)), 0.0)
    err = jnp.dot(hid, pg, preferred_element_type=F32) - own_student
    err = jnp.sum(exchange(err.astype(BF).reshape(8, 8, -1), ("co", "y")).astype(F32), 0)
    err = err + swap(err.astype(BF), "zh", 1).astype(F32)

    passage = segments[0]
    same = (passage[:, None] == passage[None, :]).astype(F32)
    weight_all = F32(512) / (COUNT * jnp.sum(same, axis=1))
    weight = lax.dynamic_slice_in_dim(weight_all, zl * 64 + core * 32 + y * 8, 8, 0)
    scaled_f = weight[:, None] * err
    student_grad = -lax.dynamic_slice_in_dim(scaled_f, zh * 4, 4, 0)
    scaled = lax.all_gather(scaled_f.astype(BF), "co")

    quarters = jnp.moveaxis(scaled.reshape(2, 8, 4, 384), 2, 0)[:, None]
    quarters = jnp.broadcast_to(quarters, (4, 4, 2, 8, 384)).reshape(16, 2, 8, 384)
    scaled_all = exchange(quarters, ("dp", "y")).reshape(4, 4, 2, 8, 384)
    scaled_all = jnp.swapaxes(scaled_all, 1, 2).reshape(256, 384)
    grad = lax.dot_general(hid_all, scaled_all, (((0,), (0,)), ((), ())), preferred_element_type=F32)
    grad = jnp.sum(exchange(grad.astype(BF).reshape(8, 64, 384), "zl").astype(F32), 0).astype(BF)
    pieces = exchange(jnp.broadcast_to(grad[None], (4, 64, 384)), "dp")
    total = jnp.concatenate([pieces[i] for i in range(4)], 1)
    factor = 1.0 / math.sqrt(512 * lax.axis_size("dp"))
    return (student_grad, total.astype(F32) * factor)


def solution(mesh):
    fine = Mesh(mesh.devices.reshape(4, 8, 2, 4, 2), ("dp", "zl", "co", "y", "zh"))
    trow, tcol = ("zl", "co"), ("y", "zh")
    in_specs = (
        P(("dp",) + tcol, trow),
        P(trow, tcol),
        P(trow, tcol),
        P("dp", tcol + trow),
        P(tcol + trow, None),
        P(("dp",) + trow + tcol, None),
        P("dp", None),
    )
    out_specs = (P(("dp",) + trow + tcol, None), P(tcol + trow, None))
    return jax.shard_map(shards, mesh=fine, in_specs=in_specs, out_specs=out_specs, check_vma=False)
```

```python
import math

import jax
import jax.numpy as jnp
from jax import lax
from jax.experimental import pallas as pl
from jax.experimental.pallas import tpu as pltpu
from jax.sharding import Mesh
from jax.sharding import PartitionSpec as P

BLOCK = 128
COUNT = 8
BF = jnp.bfloat16
F32 = jnp.float32
MIB = 1024 * 1024
VMEM = pl.BlockSpec(memory_space=pltpu.VMEM)
SMEM = pl.BlockSpec(memory_space=pltpu.SMEM)


def swap(x, axis, mask):
    return lax.ppermute(x, axis, [(i, i ^ mask) for i in range(lax.axis_size(axis))])


def pick(x, index, axis):
    return lax.dynamic_index_in_dim(x, index, axis, keepdims=False)


def exchange(x, axes):
    return lax.all_to_all(x, axes, 0, 0, tiled=True)


def gather(x, axis):
    return exchange(jnp.broadcast_to(x[None], (lax.axis_size(axis),) + x.shape), axis)


def join(x, axis, mask, bit, at):
    got = swap(x, axis, mask)
    return jnp.where(bit == 0, jnp.concatenate([x, got], at), jnp.concatenate([got, x], at))


def after(x, *others):
    return lax.optimization_barrier((x,) + others)[0]


def band_kernel(core_ref, scales_ref, weight_ref, *refs):
    *token_refs, send_ref, keep_ref, total_ref = refs
    step = pl.program_id(0)
    depth, cols = weight_ref.shape
    tokens = jnp.concatenate([r[...] for r in token_refs], 0)
    first = lax.broadcasted_iota(jnp.int32, (1, BLOCK), 1) < 64
    is_one = core_ref[0] == 1
    for m in range(2):
        tiles = []
        for j in range(4 * m, 4 * m + 4):
            column = []
            for i in range(depth // BLOCK):
                block = weight_ref[i * BLOCK : i * BLOCK + BLOCK, j * BLOCK : j * BLOCK + BLOCK].astype(F32)
                column.append((block * scales_ref[step * (depth // BLOCK) + i, j]).astype(BF))
            tiles.append(jnp.concatenate(column, 0))
        part = jnp.dot(tokens, jnp.concatenate(tiles, 1), preferred_element_type=F32)

        @pl.when(step == 0)
        def _():
            total_ref[:, 512 * m : 512 * m + 512] = part

        @pl.when(step == 1)
        def _():
            whole = total_ref[:, 512 * m : 512 * m + 512] + part
            for zp in range(2):
                a = whole[:, BLOCK * zp : BLOCK * zp + BLOCK]
                b = whole[:, BLOCK * zp + 256 : BLOCK * zp + 256 + BLOCK]
                zero = jnp.where(first, a, pltpu.roll(b, 64, 1)).astype(BF)
                one = jnp.where(first, pltpu.roll(a, 64, 1), b).astype(BF)
                at = (slice(None), pl.ds(256 * zp + BLOCK * m, BLOCK))
                send_ref[at] = jnp.where(is_one, zero, one)
                keep_ref[at] = jnp.where(is_one, one, zero)


def band(core, scales, weight, tokens):
    count, (depth, cols) = sum(v.shape[0] for v in tokens), weight.shape
    half = jax.ShapeDtypeStruct((count, cols // 2), BF)
    whole = pl.BlockSpec(half.shape, lambda k: (0, 0))
    return pl.pallas_call(
        band_kernel,
        grid=(2,),
        out_shape=(half, half),
        in_specs=[SMEM, SMEM, pl.BlockSpec((depth // 2, cols), lambda k: (k, 0))]
        + [pl.BlockSpec((v.shape[0], depth // 2), lambda k: (0, k)) for v in tokens],
        out_specs=(whole, whole),
        scratch_shapes=[pltpu.VMEM((count, cols), F32)],
        compiler_params=pltpu.CompilerParams(vmem_limit_bytes=32 * MIB),
        cost_estimate=pl.CostEstimate(flops=10**4, bytes_accessed=10**4, transcendentals=0),
    )(core.reshape(1), scales, weight, *tokens)


def combine_kernel(at_ref, near_ref, near_got_ref, far_ref, far_got_ref, res_ref, out_ref):
    y, zh = at_ref[0], at_ref[1]
    for far, (keep, got) in enumerate(((near_ref, near_got_ref), (far_ref, far_got_ref))):
        for k in range(4):
            to_y, to_z = (k, 1 - zh) if far else (y ^ k, zh)
            value = keep[k].astype(F32) + got[k].astype(F32) + res_ref[2 * to_y + to_z].astype(F32)
            for zp in range(2):
                out_ref[to_y, zp, to_z] = value[:, 256 * zp : 256 * zp + 256].astype(BF)


def combine(at, near, near_got, far, far_got, res):
    return pl.pallas_call(
        combine_kernel,
        out_shape=jax.ShapeDtypeStruct((4, 2, 2, 64, 256), BF),
        in_specs=[SMEM] + [VMEM] * 5,
        out_specs=VMEM,
        compiler_params=pltpu.CompilerParams(vmem_limit_bytes=16 * MIB),
        cost_estimate=pl.CostEstimate(flops=10**4, bytes_accessed=10**4, transcendentals=0),
    )(at, near, near_got, far, far_got, res)


def shards(hidden_in, down_weight, block_scales, residual, projector, student, segments):
    x, zq, zp, core = (lax.axis_index(name) for name in ("dp", "zq", "zp", "co"))
    y, zh = lax.axis_index("y"), lax.axis_index("zh")
    rows, cols = down_weight.shape
    half = cols // 2

    far = swap(hidden_in, "zh", 1)
    near = [hidden_in] + [swap(hidden_in, "y", k) for k in (1, 2, 3)]
    pg = join(pick(projector.reshape(4, 16, -1), x, 0)[None, None], "zq", 2, zq >> 1, 0)
    far, pg, *near = lax.optimization_barrier((far, pg, *near))
    pg = join(pg.reshape(2, 1, 16, -1), "zq", 1, zq & 1, 1).reshape(4, 1, 1, 16, -1)

    send, near = band(core, block_scales, down_weight, near)
    near_got = swap(send, "co", 1)
    far, pg = lax.optimization_barrier((gather(far, "y").reshape(256, rows), pg))
    send, far = band(core, block_scales, down_weight, [far])
    far_got = swap(send, "co", 1)

    pg = join(pg, "dp", 1, x & 1, 2)
    pg = join(pg, "dp", 2, x >> 1, 1).reshape(256, -1)

    column = jnp.arange(half)[None, :]
    place = (column == zp * 256 + zq * 64 + jnp.arange(64)[:, None]).astype(BF)
    res = jnp.dot(residual, place, preferred_element_type=F32).astype(BF).reshape(8, 64, half)
    blocks = lambda v: v.reshape(4, 64, half)
    acc = combine(jnp.stack([y, zh]), blocks(near), blocks(near_got), blocks(far), blocks(far_got), res)
    hid = exchange(acc.reshape(8, BLOCK, 256), ("zq", "zp"))
    hid = jnp.sum(hid.astype(F32), 0).astype(BF)

    mine = (jnp.arange(BLOCK) // 4 == zp * 16 + core * 8 + y * 2 + zh)[:, None]
    own_student = jnp.where(mine, jnp.tile(student.astype(F32), (32, 1)), 0.0)
    err = jnp.dot(hid, pg, preferred_element_type=F32) - own_student
    err = jnp.sum(exchange(err.astype(BF).reshape(16, 8, -1), ("zp", "co", "y")).astype(F32), 0)
    hid_two = after(jnp.stack([hid, swap(hid, "dp", 1)]), err)
    hid_all = jnp.concatenate([hid_two, swap(hid_two, "dp", 2)])
    hid_all = jnp.take(hid_all, x ^ jnp.arange(4), axis=0).reshape(512, 256)
    err = err + swap(err.astype(BF), "zh", 1).astype(F32)

    passage = segments[0]
    same = (passage[:, None] == passage[None, :]).astype(F32)
    weight_all = F32(512) / (COUNT * jnp.sum(same, axis=1))
    weight = lax.dynamic_slice_in_dim(weight_all, zq * 128 + zp * 64 + core * 32 + y * 8, 8, 0)
    scaled_f = weight[:, None] * err
    student_grad = -lax.dynamic_slice_in_dim(scaled_f, zh * 4, 4, 0)
    scaled = lax.all_gather(scaled_f.astype(BF), ("zp", "co"))

    quarters = jnp.moveaxis(scaled.reshape(4, 8, 4, 384), 2, 0)[:, None]
    quarters = jnp.broadcast_to(quarters, (4, 4, 4, 8, 384)).reshape(16, 4, 8, 384)
    scaled_all = exchange(quarters, ("dp", "y")).reshape(4, 4, 4, 8, 384)
    scaled_all = jnp.swapaxes(scaled_all, 1, 2).reshape(512, 384)
    grad = lax.dot_general(hid_all, scaled_all, (((0,), (0,)), ((), ())), preferred_element_type=F32)
    grad = jnp.sum(exchange(grad.astype(BF).reshape(4, 64, 384), "zq").astype(F32), 0).astype(BF)
    pieces = gather(grad, "dp").reshape(4, 64, 384)
    total = jnp.concatenate([pieces[i] for i in range(4)], 1)
    factor = 1.0 / math.sqrt(512 * lax.axis_size("dp"))
    return (student_grad, total.astype(F32) * factor)


def solution(mesh):
    names = ("dp", "zq", "zp", "co", "y", "zh")
    fine = Mesh(mesh.devices.reshape(4, 4, 2, 2, 4, 2), names)
    trow, tcol = names[1:4], names[4:]
    in_specs = (
        P(("dp",) + tcol, trow),
        P(trow, tcol),
        P(trow, tcol),
        P("dp", tcol + trow),
        P(tcol + trow, None),
        P(("dp",) + trow + tcol, None),
        P("dp", None),
    )
    out_specs = (P(("dp",) + trow + tcol, None), P(tcol + trow, None))
    return jax.shard_map(shards, mesh=fine, in_specs=in_specs, out_specs=out_specs, check_vma=False)
```

```python
import math

import jax
import jax.numpy as jnp
from jax import lax
from jax.experimental import pallas as pl
from jax.experimental.pallas import tpu as pltpu
from jax.sharding import Mesh
from jax.sharding import PartitionSpec as P

BLOCK = 128
COUNT = 8
BF = jnp.bfloat16
F32 = jnp.float32
MIB = 1024 * 1024
VMEM = pl.BlockSpec(memory_space=pltpu.VMEM)
SMEM = pl.BlockSpec(memory_space=pltpu.SMEM)
COST = pl.CostEstimate(flops=10**4, bytes_accessed=10**4, transcendentals=0)


def swap(x, axis, mask):
    return lax.ppermute(x, axis, [(i, i ^ mask) for i in range(lax.axis_size(axis))])


def pick(x, index, axis):
    return lax.dynamic_index_in_dim(x, index, axis, keepdims=False)


def exchange(x, axes):
    return lax.all_to_all(x, axes, 0, 0, tiled=True)


def gather(x, axis):
    return exchange(jnp.broadcast_to(x[None], (lax.axis_size(axis),) + x.shape), axis)


def placed(x, got, bit, at):
    return jnp.where(bit == 0, jnp.concatenate([x, got], at), jnp.concatenate([got, x], at))


def join(x, axis, mask, bit, at):
    return placed(x, swap(x, axis, mask), bit, at)


def after(x, *others):
    return lax.optimization_barrier((x,) + others)[0]


def scale_kernel(scales_ref, weight_ref, out_ref):
    rows, cols = weight_ref.shape
    for j in range(cols // BLOCK):
        for i in range(rows // BLOCK):
            at = (pl.ds(i * BLOCK, BLOCK), pl.ds(j * BLOCK, BLOCK))
            out_ref[at] = (weight_ref[at].astype(F32) * scales_ref[j, i]).astype(BF)


def scale(weight, scales):
    return pl.pallas_call(
        scale_kernel,
        out_shape=jax.ShapeDtypeStruct(weight.shape, BF),
        in_specs=[SMEM, VMEM],
        out_specs=VMEM,
        compiler_params=pltpu.CompilerParams(vmem_limit_bytes=24 * MIB),
        cost_estimate=COST,
    )(scales, weight)


def band_kernel(core_ref, weight_ref, *refs):
    *token_refs, send_ref, keep_ref = refs
    tokens = jnp.concatenate([r[...] for r in token_refs], 0)
    first = lax.broadcasted_iota(jnp.int32, (1, BLOCK), 1) < 64
    is_one = core_ref[0] == 1
    for m in range(2):
        part = jnp.dot(tokens, weight_ref[:, 512 * m : 512 * m + 512], preferred_element_type=F32)
        for zp in range(2):
            a = part[:, BLOCK * zp : BLOCK * zp + BLOCK]
            b = part[:, BLOCK * zp + 256 : BLOCK * zp + 256 + BLOCK]
            zero = jnp.where(first, a, pltpu.roll(b, 64, 1)).astype(BF)
            one = jnp.where(first, pltpu.roll(a, 64, 1), b).astype(BF)
            at = (slice(None), pl.ds(256 * zp + BLOCK * m, BLOCK))
            send_ref[at] = jnp.where(is_one, zero, one)
            keep_ref[at] = jnp.where(is_one, one, zero)


def band(core, weight, tokens):
    rows = sum(v.shape[0] for v in tokens)
    half = jax.ShapeDtypeStruct((rows, weight.shape[1] // 2), BF)
    return pl.pallas_call(
        band_kernel,
        out_shape=(half, half),
        in_specs=[SMEM] + [VMEM] * (1 + len(tokens)),
        out_specs=(VMEM, VMEM),
        compiler_params=pltpu.CompilerParams(vmem_limit_bytes=24 * MIB),
        cost_estimate=COST,
    )(core.reshape(1), weight, *tokens)


def combine_kernel(at_ref, near_ref, near_got_ref, far_ref, far_got_ref, res_ref, out_ref):
    y, zh = at_ref[0], at_ref[1]
    for far, (keep, got) in enumerate(((near_ref, near_got_ref), (far_ref, far_got_ref))):
        for k in range(4):
            to_y, to_z = (k, 1 - zh) if far else (y ^ k, zh)
            value = keep[k].astype(F32) + got[k].astype(F32) + res_ref[2 * to_y + to_z].astype(F32)
            for zp in range(2):
                out_ref[to_y, zp, to_z] = value[:, 256 * zp : 256 * zp + 256].astype(BF)


def combine(at, near, near_got, far, far_got, res):
    return pl.pallas_call(
        combine_kernel,
        out_shape=jax.ShapeDtypeStruct((4, 2, 2, 64, 256), BF),
        in_specs=[SMEM] + [VMEM] * 5,
        out_specs=VMEM,
        compiler_params=pltpu.CompilerParams(vmem_limit_bytes=16 * MIB),
        cost_estimate=COST,
    )(at, near, near_got, far, far_got, res)


def shards(hidden_in, down_weight, block_scales, residual, projector, student, segments):
    x, zq, zp, core = (lax.axis_index(name) for name in ("dp", "zq", "zp", "co"))
    y, zh = lax.axis_index("y"), lax.axis_index("zh")
    rows, cols = down_weight.shape
    half = cols // 2

    far = swap(hidden_in, "zh", 1)
    near = [hidden_in] + [swap(hidden_in, "y", k) for k in (1, 2, 3)]
    effective = scale(down_weight, block_scales.T)

    pg = pick(projector.reshape(4, 16, -1), x, 0)[None, None]
    got = swap(pg, "zq", 2)
    far, got, effective, *near = lax.optimization_barrier((far, got, effective, *near))
    pg = placed(pg, got, zq >> 1, 0)
    pg = join(pg.reshape(2, 1, 16, -1), "zq", 1, zq & 1, 1).reshape(4, 1, 1, 16, -1)

    send, near = band(core, effective, near)
    near_got = swap(send, "co", 1)
    far, pg = lax.optimization_barrier((gather(far, "y").reshape(256, rows), pg))
    send, far = band(core, effective, [far])
    far_got = swap(send, "co", 1)

    pg = join(pg, "dp", 1, x & 1, 2)
    pg = join(pg, "dp", 2, x >> 1, 1).reshape(256, -1)

    column = jnp.arange(half)[None, :]
    place = (column == zp * 256 + zq * 64 + jnp.arange(64)[:, None]).astype(BF)
    res = jnp.dot(residual, place, preferred_element_type=F32).astype(BF).reshape(8, 64, half)
    blocks = lambda v: v.reshape(4, 64, half)
    acc = combine(jnp.stack([y, zh]), blocks(near), blocks(near_got), blocks(far), blocks(far_got), res)
    hid = exchange(acc.reshape(8, BLOCK, 256), ("zq", "zp"))
    hid = jnp.sum(hid.astype(F32), 0).astype(BF)

    mine = (jnp.arange(BLOCK) // 4 == zp * 16 + core * 8 + y * 2 + zh)[:, None]
    own_student = jnp.where(mine, jnp.tile(student.astype(F32), (32, 1)), 0.0)
    err = jnp.dot(hid, pg, preferred_element_type=F32) - own_student
    err = jnp.sum(exchange(err.astype(BF).reshape(16, 8, -1), ("zp", "co", "y")).astype(F32), 0)
    hid_two = after(jnp.stack([hid, swap(hid, "dp", 1)]), err)
    hid_all = jnp.concatenate([hid_two, swap(hid_two, "dp", 2)])
    hid_all = jnp.take(hid_all, x ^ jnp.arange(4), axis=0).reshape(512, 256)
    err = err + swap(err.astype(BF), "zh", 1).astype(F32)

    passage = segments[0]
    same = (passage[:, None] == passage[None, :]).astype(F32)
    weight_all = F32(512) / (COUNT * jnp.sum(same, axis=1))
    weight = lax.dynamic_slice_in_dim(weight_all, zq * 128 + zp * 64 + core * 32 + y * 8, 8, 0)
    scaled_f = weight[:, None] * err
    student_grad = -lax.dynamic_slice_in_dim(scaled_f, zh * 4, 4, 0)
    scaled = lax.all_gather(scaled_f.astype(BF), ("zp", "co"))

    quarters = jnp.moveaxis(scaled.reshape(4, 8, 4, 384), 2, 0)[:, None]
    quarters = jnp.broadcast_to(quarters, (4, 4, 4, 8, 384)).reshape(16, 4, 8, 384)
    scaled_all = exchange(quarters, ("dp", "y")).reshape(4, 4, 4, 8, 384)
    scaled_all = jnp.swapaxes(scaled_all, 1, 2).reshape(512, 384)
    grad = lax.dot_general(hid_all, scaled_all, (((0,), (0,)), ((), ())), preferred_element_type=F32)
    grad = jnp.sum(exchange(grad.astype(BF).reshape(4, 64, 384), "zq").astype(F32), 0).astype(BF)
    pieces = gather(grad, "dp").reshape(4, 64, 384)
    total = jnp.concatenate([pieces[i] for i in range(4)], 1)
    factor = 1.0 / math.sqrt(512 * lax.axis_size("dp"))
    return (student_grad, total.astype(F32) * factor)


def solution(mesh):
    names = ("dp", "zq", "zp", "co", "y", "zh")
    fine = Mesh(mesh.devices.reshape(4, 4, 2, 2, 4, 2), names)
    trow, tcol = names[1:4], names[4:]
    in_specs = (
        P(("dp",) + tcol, trow),
        P(trow, tcol),
        P(trow, tcol),
        P("dp", tcol + trow),
        P(tcol + trow, None),
        P(("dp",) + trow + tcol, None),
        P("dp", None),
    )
    out_specs = (P(("dp",) + trow + tcol, None), P(tcol + trow, None))
    return jax.shard_map(shards, mesh=fine, in_specs=in_specs, out_specs=out_specs, check_vma=False)
```

```python
import math

import jax
import jax.numpy as jnp
from jax import lax
from jax.experimental import pallas as pl
from jax.experimental.pallas import tpu as pltpu
from jax.sharding import Mesh
from jax.sharding import PartitionSpec as P

BLOCK = 128
COUNT = 8
BF = jnp.bfloat16
F32 = jnp.float32
MIB = 1024 * 1024
VMEM = pl.BlockSpec(memory_space=pltpu.VMEM)
SMEM = pl.BlockSpec(memory_space=pltpu.SMEM)
COST = pl.CostEstimate(flops=10**4, bytes_accessed=10**4, transcendentals=0)


def swap(x, axis, mask):
    return lax.ppermute(x, axis, [(i, i ^ mask) for i in range(lax.axis_size(axis))])


def pick(x, index, axis):
    return lax.dynamic_index_in_dim(x, index, axis, keepdims=False)


def exchange(x, axes):
    return lax.all_to_all(x, axes, 0, 0, tiled=True)


def gather(x, axis):
    return exchange(jnp.broadcast_to(x[None], (lax.axis_size(axis),) + x.shape), axis)


def placed(x, got, bit, at):
    return jnp.where(bit == 0, jnp.concatenate([x, got], at), jnp.concatenate([got, x], at))


def join(x, axis, mask, bit, at):
    return placed(x, swap(x, axis, mask), bit, at)


def after(x, *others):
    return lax.optimization_barrier((x,) + others)[0]


def scale_kernel(scales_ref, weight_ref, out_ref):
    rows, cols = weight_ref.shape
    for j in range(cols // BLOCK):
        for i in range(rows // BLOCK):
            at = (pl.ds(i * BLOCK, BLOCK), pl.ds(j * BLOCK, BLOCK))
            out_ref[at] = (weight_ref[at].astype(F32) * scales_ref[j, i]).astype(BF)


def scale(weight, scales):
    return pl.pallas_call(
        scale_kernel,
        out_shape=jax.ShapeDtypeStruct(weight.shape, BF),
        in_specs=[SMEM, VMEM],
        out_specs=VMEM,
        compiler_params=pltpu.CompilerParams(vmem_limit_bytes=24 * MIB),
        cost_estimate=COST,
    )(scales, weight)


def band_kernel(core_ref, weight_ref, *refs):
    *token_refs, send_ref, keep_ref = refs
    tokens = jnp.concatenate([r[...] for r in token_refs], 0)
    first = lax.broadcasted_iota(jnp.int32, (1, BLOCK), 1) < 64
    is_one = core_ref[0] == 1
    for m in range(2):
        part = jnp.dot(tokens, weight_ref[:, 512 * m : 512 * m + 512], preferred_element_type=F32)
        for zp in range(2):
            a = part[:, BLOCK * zp : BLOCK * zp + BLOCK]
            b = part[:, BLOCK * zp + 256 : BLOCK * zp + 256 + BLOCK]
            zero = jnp.where(first, a, pltpu.roll(b, 64, 1)).astype(BF)
            one = jnp.where(first, pltpu.roll(a, 64, 1), b).astype(BF)
            at = (slice(None), pl.ds(256 * zp + BLOCK * m, BLOCK))
            send_ref[at] = jnp.where(is_one, zero, one)
            keep_ref[at] = jnp.where(is_one, one, zero)


def band(core, weight, tokens):
    rows = sum(v.shape[0] for v in tokens)
    half = jax.ShapeDtypeStruct((rows, weight.shape[1] // 2), BF)
    return pl.pallas_call(
        band_kernel,
        out_shape=(half, half),
        in_specs=[SMEM] + [VMEM] * (1 + len(tokens)),
        out_specs=(VMEM, VMEM),
        compiler_params=pltpu.CompilerParams(vmem_limit_bytes=24 * MIB),
        cost_estimate=COST,
    )(core.reshape(1), weight, *tokens)


def combine_kernel(at_ref, near_ref, near_got_ref, far_ref, far_got_ref, res_ref, out_ref):
    y, zh = at_ref[0], at_ref[1]
    for far, (keep, got) in enumerate(((near_ref, near_got_ref), (far_ref, far_got_ref))):
        for k in range(4):
            to_y, to_z = (k, 1 - zh) if far else (y ^ k, zh)
            value = keep[k].astype(F32) + got[k].astype(F32) + res_ref[2 * to_y + to_z].astype(F32)
            for zp in range(2):
                out_ref[to_y, zp, to_z] = value[:, 256 * zp : 256 * zp + 256].astype(BF)


def combine(at, near, near_got, far, far_got, res):
    return pl.pallas_call(
        combine_kernel,
        out_shape=jax.ShapeDtypeStruct((4, 2, 2, 64, 256), BF),
        in_specs=[SMEM] + [VMEM] * 5,
        out_specs=VMEM,
        compiler_params=pltpu.CompilerParams(vmem_limit_bytes=16 * MIB),
        cost_estimate=COST,
    )(at, near, near_got, far, far_got, res)


def shards(hidden_in, down_weight, block_scales, residual, projector, student, segments):
    x, zq, zp, core = (lax.axis_index(name) for name in ("dp", "zq", "zp", "co"))
    y, zh = lax.axis_index("y"), lax.axis_index("zh")
    rows, cols = down_weight.shape
    half = cols // 2

    far = swap(hidden_in, "zh", 1)
    near = [hidden_in] + [swap(hidden_in, "y", k) for k in (1, 2, 3)]
    effective = scale(down_weight, block_scales.T)

    pg = pick(projector.reshape(4, 16, -1), x, 0)[None, None]
    got = swap(pg, "zq", 2)
    far, got, effective, *near = lax.optimization_barrier((far, got, effective, *near))
    pg = placed(pg, got, zq >> 1, 0)
    pg = join(pg.reshape(2, 1, 16, -1), "zq", 1, zq & 1, 1).reshape(4, 1, 1, 16, -1)

    send, near = band(core, effective, near)
    near_got = swap(send, "co", 1)
    far, pg = lax.optimization_barrier((gather(far, "y").reshape(256, rows), pg))
    send, far = band(core, effective, [far])
    far_got = swap(send, "co", 1)

    pg = join(pg, "dp", 1, x & 1, 2)
    pg = join(pg, "dp", 2, x >> 1, 1).reshape(256, -1)

    column = jnp.arange(half)[None, :]
    place = (column == zp * 256 + zq * 64 + jnp.arange(64)[:, None]).astype(BF)
    res = jnp.dot(residual, place, preferred_element_type=F32).astype(BF).reshape(8, 64, half)
    blocks = lambda v: v.reshape(4, 64, half)
    acc = combine(jnp.stack([y, zh]), blocks(near), blocks(near_got), blocks(far), blocks(far_got), res)
    hid = exchange(acc.reshape(8, BLOCK, 256), ("zq", "zp"))
    hid = jnp.sum(hid.astype(F32), 0).astype(BF)

    mine = (jnp.arange(BLOCK) // 4 == zp * 16 + core * 8 + y * 2 + zh)[:, None]
    own_student = jnp.where(mine, jnp.tile(student.astype(F32), (32, 1)), 0.0)
    err = jnp.dot(hid, pg, preferred_element_type=F32) - own_student
    err = jnp.sum(exchange(err.astype(BF).reshape(16, 8, -1), ("zp", "co", "y")).astype(F32), 0)
    hid_two = after(jnp.stack([hid, swap(hid, "dp", 1)]), err)
    hid_all = jnp.concatenate([hid_two, swap(hid_two, "dp", 2)])
    hid_all = jnp.take(hid_all, x ^ jnp.arange(4), axis=0).reshape(512, 256)
    err = err + swap(err.astype(BF), "zh", 1).astype(F32)
    err, hid_all = lax.optimization_barrier((err, hid_all))

    passage = segments[0]
    same = (passage[:, None] == passage[None, :]).astype(F32)
    weight_all = F32(512) / (COUNT * jnp.sum(same, axis=1))
    weight = lax.dynamic_slice_in_dim(weight_all, zq * 128 + zp * 64 + core * 32 + y * 8, 8, 0)
    scaled_f = weight[:, None] * err
    student_grad = -lax.dynamic_slice_in_dim(scaled_f, zh * 4, 4, 0)
    scaled = lax.all_gather(scaled_f.astype(BF), "co")

    quarters = jnp.moveaxis(scaled.reshape(2, 8, 4, 384), 2, 0)[:, None]
    quarters = jnp.broadcast_to(quarters, (4, 8, 2, 8, 384)).reshape(32, 2, 8, 384)
    scaled_all = exchange(quarters, ("dp", "zp", "y")).reshape(8, 4, 2, 8, 384)
    scaled_all = jnp.swapaxes(scaled_all, 1, 2).reshape(512, 384)
    grad = lax.dot_general(hid_all, scaled_all, (((0,), (0,)), ((), ())), preferred_element_type=F32)
    grad = jnp.sum(exchange(grad.astype(BF).reshape(4, 64, 384), "zq").astype(F32), 0).astype(BF)
    pieces = gather(grad, "dp").reshape(4, 64, 384)
    total = jnp.concatenate([pieces[i] for i in range(4)], 1)
    factor = 1.0 / math.sqrt(512 * lax.axis_size("dp"))
    return (student_grad, total.astype(F32) * factor)


def solution(mesh):
    names = ("dp", "zq", "zp", "co", "y", "zh")
    fine = Mesh(mesh.devices.reshape(4, 4, 2, 2, 4, 2), names)
    trow, tcol = names[1:4], names[4:]
    in_specs = (
        P(("dp",) + tcol, trow),
        P(trow, tcol),
        P(trow, tcol),
        P("dp", tcol + trow),
        P(tcol + trow, None),
        P(("dp",) + trow + tcol, None),
        P("dp", None),
    )
    out_specs = (P(("dp",) + trow + tcol, None), P(tcol + trow, None))
    return jax.shard_map(shards, mesh=fine, in_specs=in_specs, out_specs=out_specs, check_vma=False)
```

```python
import math

import jax
import jax.numpy as jnp
from jax import lax
from jax.experimental import pallas as pl
from jax.experimental.pallas import tpu as pltpu
from jax.sharding import Mesh
from jax.sharding import PartitionSpec as P

BLOCK = 128
COUNT = 8
BF = jnp.bfloat16
F32 = jnp.float32
MIB = 1024 * 1024
VMEM = pl.BlockSpec(memory_space=pltpu.VMEM)
SMEM = pl.BlockSpec(memory_space=pltpu.SMEM)
COST = pl.CostEstimate(flops=10**4, bytes_accessed=10**4, transcendentals=0)


def swap(x, axis, mask):
    return lax.ppermute(x, axis, [(i, i ^ mask) for i in range(lax.axis_size(axis))])


def pick(x, index, axis):
    return lax.dynamic_index_in_dim(x, index, axis, keepdims=False)


def exchange(x, axes):
    return lax.all_to_all(x, axes, 0, 0, tiled=True)


def gather(x, axis):
    return exchange(jnp.broadcast_to(x[None], (lax.axis_size(axis),) + x.shape), axis)


def placed(x, got, bit, at):
    return jnp.where(bit == 0, jnp.concatenate([x, got], at), jnp.concatenate([got, x], at))


def join(x, axis, mask, bit, at):
    return placed(x, swap(x, axis, mask), bit, at)


def after(x, *others):
    return lax.optimization_barrier((x,) + others)[0]


def scale_kernel(scales_ref, weight_ref, out_ref):
    rows, cols = weight_ref.shape
    for j in range(cols // BLOCK):
        for i in range(rows // BLOCK):
            at = (pl.ds(i * BLOCK, BLOCK), pl.ds(j * BLOCK, BLOCK))
            out_ref[at] = (weight_ref[at].astype(F32) * scales_ref[j, i]).astype(BF)


def scale(weight, scales):
    return pl.pallas_call(
        scale_kernel,
        out_shape=jax.ShapeDtypeStruct(weight.shape, BF),
        in_specs=[SMEM, VMEM],
        out_specs=VMEM,
        compiler_params=pltpu.CompilerParams(vmem_limit_bytes=24 * MIB),
        cost_estimate=COST,
    )(scales, weight)


def band_kernel(core_ref, weight_ref, *refs):
    *token_refs, send_ref, keep_ref = refs
    tokens = jnp.concatenate([r[...] for r in token_refs], 0)
    first = lax.broadcasted_iota(jnp.int32, (1, BLOCK), 1) < 64
    is_one = core_ref[0] == 1
    for m in range(2):
        part = jnp.dot(tokens, weight_ref[:, 512 * m : 512 * m + 512], preferred_element_type=F32)
        for zp in range(2):
            a = part[:, BLOCK * zp : BLOCK * zp + BLOCK]
            b = part[:, BLOCK * zp + 256 : BLOCK * zp + 256 + BLOCK]
            zero = jnp.where(first, a, pltpu.roll(b, 64, 1)).astype(BF)
            one = jnp.where(first, pltpu.roll(a, 64, 1), b).astype(BF)
            at = (slice(None), pl.ds(256 * zp + BLOCK * m, BLOCK))
            send_ref[at] = jnp.where(is_one, zero, one)
            keep_ref[at] = jnp.where(is_one, one, zero)


def band(core, weight, tokens):
    rows = sum(v.shape[0] for v in tokens)
    half = jax.ShapeDtypeStruct((rows, weight.shape[1] // 2), BF)
    return pl.pallas_call(
        band_kernel,
        out_shape=(half, half),
        in_specs=[SMEM] + [VMEM] * (1 + len(tokens)),
        out_specs=(VMEM, VMEM),
        compiler_params=pltpu.CompilerParams(vmem_limit_bytes=24 * MIB),
        cost_estimate=COST,
    )(core.reshape(1), weight, *tokens)


def combine_kernel(at_ref, near_ref, near_got_ref, far_ref, far_got_ref, res_ref, out_ref):
    y, zh = at_ref[0], at_ref[1]
    for far, (keep, got) in enumerate(((near_ref, near_got_ref), (far_ref, far_got_ref))):
        for k in range(4):
            at, to_z = (k, 1 - zh) if far else (y ^ k, zh)
            value = keep[at].astype(F32) + got[at].astype(F32) + res_ref[2 * k + to_z].astype(F32)
            for zp in range(2):
                out_ref[k, zp, to_z] = value[:, 256 * zp : 256 * zp + 256].astype(BF)


def combine(at, near, near_got, far, far_got, res):
    return pl.pallas_call(
        combine_kernel,
        out_shape=jax.ShapeDtypeStruct((4, 2, 2, 64, 256), BF),
        in_specs=[SMEM] + [VMEM] * 5,
        out_specs=VMEM,
        compiler_params=pltpu.CompilerParams(vmem_limit_bytes=16 * MIB),
        cost_estimate=COST,
    )(at, near, near_got, far, far_got, res)


def shards(hidden_in, down_weight, block_scales, residual, projector, student, segments):
    x, zq, zp, core = (lax.axis_index(name) for name in ("dp", "zq", "zp", "co"))
    y, zh = lax.axis_index("y"), lax.axis_index("zh")
    rows, cols = down_weight.shape
    half = cols // 2

    far = swap(hidden_in, "zh", 1)
    near = [hidden_in] + [swap(hidden_in, "y", k) for k in (1, 2, 3)]
    effective = scale(down_weight, block_scales.T)

    pg = pick(projector.reshape(4, 16, -1), x, 0)[None, None]
    got = swap(pg, "zq", 2)
    far, got, effective, *near = lax.optimization_barrier((far, got, effective, *near))
    pg = placed(pg, got, zq >> 1, 0)
    pg = join(pg.reshape(2, 1, 16, -1), "zq", 1, zq & 1, 1).reshape(4, 1, 1, 16, -1)

    send, near = band(core, effective, near)
    near_got = swap(send, "co", 1)
    far, pg = lax.optimization_barrier((gather(far, "y").reshape(256, rows), pg))
    send, far = band(core, effective, [far])
    far_got = swap(send, "co", 1)

    pg = join(pg, "dp", 1, x & 1, 2)
    pg = join(pg, "dp", 2, x >> 1, 1).reshape(256, -1)

    column = jnp.arange(half)[None, :]
    place = (column == zp * 256 + zq * 64 + jnp.arange(64)[:, None]).astype(BF)
    res = jnp.dot(residual, place, preferred_element_type=F32).astype(BF).reshape(8, 64, half)
    blocks = lambda v: v.reshape(4, 64, half)
    acc = combine(jnp.stack([y, zh]), blocks(near), blocks(near_got), blocks(far), blocks(far_got), res)
    hid = exchange(acc.reshape(8, BLOCK, 256), ("zq", "zp"))
    hid = jnp.sum(hid.astype(F32), 0).astype(BF)

    mine = (jnp.arange(BLOCK) // 4 == zp * 16 + core * 8 + y * 2 + zh)[:, None]
    own_student = jnp.where(mine, jnp.tile(student.astype(F32), (32, 1)), 0.0)
    err = jnp.dot(hid, pg, preferred_element_type=F32) - own_student
    err = jnp.sum(exchange(err.astype(BF).reshape(16, 8, -1), ("zp", "co", "y")).astype(F32), 0)
    hid_two = after(jnp.stack([hid, swap(hid, "dp", 1)]), err)
    hid_got = swap(hid_two, "dp", 2)
    err = err + swap(err.astype(BF), "zh", 1).astype(F32)
    err, hid_got = lax.optimization_barrier((err, hid_got))
    hid_two = placed(hid_two[:1], hid_two[1:], x & 1, 0)
    hid_all = placed(hid_two, placed(hid_got[:1], hid_got[1:], x & 1, 0), x >> 1, 0).reshape(512, 256)

    passage = segments[0]
    same = (passage[:, None] == passage[None, :]).astype(F32)
    weight_all = F32(512) / (COUNT * jnp.sum(same, axis=1))
    weight = lax.dynamic_slice_in_dim(weight_all, zq * 128 + zp * 64 + core * 32 + y * 8, 8, 0)
    scaled_f = weight[:, None] * err
    student_grad = -lax.dynamic_slice_in_dim(scaled_f, zh * 4, 4, 0)
    scaled = lax.all_gather(scaled_f.astype(BF), "co")

    quarters = jnp.moveaxis(scaled.reshape(2, 8, 4, 384), 2, 0)[:, None]
    quarters = jnp.broadcast_to(quarters, (4, 8, 2, 8, 384)).reshape(32, 2, 8, 384)
    scaled_all = exchange(quarters, ("dp", "zp", "y")).reshape(8, 4, 2, 8, 384)
    scaled_all = jnp.swapaxes(scaled_all, 1, 2).reshape(512, 384)
    grad = lax.dot_general(hid_all, scaled_all, (((0,), (0,)), ((), ())), preferred_element_type=F32)
    grad = jnp.sum(exchange(grad.astype(BF).reshape(4, 64, 384), "zq").astype(F32), 0).astype(BF)
    pieces = gather(grad, "dp").reshape(4, 64, 384)
    total = jnp.concatenate([pieces[i] for i in range(4)], 1)
    factor = 1.0 / math.sqrt(512 * lax.axis_size("dp"))
    return (student_grad, total.astype(F32) * factor)


def solution(mesh):
    names = ("dp", "zq", "zp", "co", "y", "zh")
    fine = Mesh(mesh.devices.reshape(4, 4, 2, 2, 4, 2), names)
    trow, tcol = names[1:4], names[4:]
    in_specs = (
        P(("dp",) + tcol, trow),
        P(trow, tcol),
        P(trow, tcol),
        P("dp", tcol + trow),
        P(tcol + trow, None),
        P(("dp",) + trow + tcol, None),
        P("dp", None),
    )
    out_specs = (P(("dp",) + trow + tcol, None), P(tcol + trow, None))
    return jax.shard_map(shards, mesh=fine, in_specs=in_specs, out_specs=out_specs, check_vma=False)
```

```python
import math

import jax
import jax.numpy as jnp
from jax import lax
from jax.experimental import pallas as pl
from jax.experimental.pallas import tpu as pltpu
from jax.sharding import Mesh
from jax.sharding import PartitionSpec as P

BLOCK = 128
COUNT = 8
BF = jnp.bfloat16
F32 = jnp.float32
MIB = 1024 * 1024
VMEM = pl.BlockSpec(memory_space=pltpu.VMEM)
SMEM = pl.BlockSpec(memory_space=pltpu.SMEM)
COST = pl.CostEstimate(flops=10**4, bytes_accessed=10**4, transcendentals=0)


def swap(x, axis, mask):
    return lax.ppermute(x, axis, [(i, i ^ mask) for i in range(lax.axis_size(axis))])


def pick(x, index, axis):
    return lax.dynamic_index_in_dim(x, index, axis, keepdims=False)


def exchange(x, axes):
    return lax.all_to_all(x, axes, 0, 0, tiled=True)


def gather(x, axis):
    return exchange(jnp.broadcast_to(x[None], (lax.axis_size(axis),) + x.shape), axis)


def placed(x, got, bit, at):
    return jnp.where(bit == 0, jnp.concatenate([x, got], at), jnp.concatenate([got, x], at))


def join(x, axis, mask, bit, at):
    return placed(x, swap(x, axis, mask), bit, at)


def after(x, *others):
    return lax.optimization_barrier((x,) + others)[0]


def scale_kernel(scales_ref, weight_ref, out_ref):
    rows, cols = weight_ref.shape
    for j in range(cols // BLOCK):
        for i in range(rows // BLOCK):
            at = (pl.ds(i * BLOCK, BLOCK), pl.ds(j * BLOCK, BLOCK))
            out_ref[at] = (weight_ref[at].astype(F32) * scales_ref[j, i]).astype(BF)


def scale(weight, scales):
    return pl.pallas_call(
        scale_kernel,
        out_shape=jax.ShapeDtypeStruct(weight.shape, BF),
        in_specs=[SMEM, VMEM],
        out_specs=VMEM,
        compiler_params=pltpu.CompilerParams(vmem_limit_bytes=24 * MIB),
        cost_estimate=COST,
    )(scales, weight)


def band_kernel(core_ref, weight_ref, *refs):
    *token_refs, send_ref, keep_ref = refs
    tokens = jnp.concatenate([r[...] for r in token_refs], 0)
    first = lax.broadcasted_iota(jnp.int32, (1, BLOCK), 1) < 64
    is_one = core_ref[0] == 1
    for m in range(2):
        part = jnp.dot(tokens, weight_ref[:, 512 * m : 512 * m + 512], preferred_element_type=F32)
        for zp in range(2):
            a = part[:, BLOCK * zp : BLOCK * zp + BLOCK]
            b = part[:, BLOCK * zp + 256 : BLOCK * zp + 256 + BLOCK]
            zero = jnp.where(first, a, pltpu.roll(b, 64, 1)).astype(BF)
            one = jnp.where(first, pltpu.roll(a, 64, 1), b).astype(BF)
            at = (slice(None), pl.ds(256 * zp + BLOCK * m, BLOCK))
            send_ref[at] = jnp.where(is_one, zero, one)
            keep_ref[at] = jnp.where(is_one, one, zero)


def band(core, weight, tokens):
    rows = sum(v.shape[0] for v in tokens)
    half = jax.ShapeDtypeStruct((rows, weight.shape[1] // 2), BF)
    return pl.pallas_call(
        band_kernel,
        out_shape=(half, half),
        in_specs=[SMEM] + [VMEM] * (1 + len(tokens)),
        out_specs=(VMEM, VMEM),
        compiler_params=pltpu.CompilerParams(vmem_limit_bytes=24 * MIB),
        cost_estimate=COST,
    )(core.reshape(1), weight, *tokens)


def combine_kernel(at_ref, near_ref, near_got_ref, far_ref, far_got_ref, res_ref, out_ref):
    y, zh = at_ref[0], at_ref[1]
    for far, (keep, got) in enumerate(((near_ref, near_got_ref), (far_ref, far_got_ref))):
        for k in range(4):
            to_y, to_z = (k, 1 - zh) if far else (y ^ k, zh)
            value = keep[k].astype(F32) + got[k].astype(F32) + res_ref[2 * to_y + to_z].astype(F32)
            for zp in range(2):
                out_ref[to_y, zp, to_z] = value[:, 256 * zp : 256 * zp + 256].astype(BF)


def combine(at, near, near_got, far, far_got, res):
    return pl.pallas_call(
        combine_kernel,
        out_shape=jax.ShapeDtypeStruct((4, 2, 2, 64, 256), BF),
        in_specs=[SMEM] + [VMEM] * 5,
        out_specs=VMEM,
        compiler_params=pltpu.CompilerParams(vmem_limit_bytes=16 * MIB),
        cost_estimate=COST,
    )(at, near, near_got, far, far_got, res)


def shards(hidden_in, down_weight, block_scales, residual, projector, student, segments):
    x, zq, zp, core = (lax.axis_index(name) for name in ("dp", "zq", "zp", "co"))
    y, zh = lax.axis_index("y"), lax.axis_index("zh")
    rows, cols = down_weight.shape
    half = cols // 2

    far = swap(hidden_in, "zh", 1)
    near = [hidden_in] + [swap(hidden_in, "y", k) for k in (1, 2, 3)]
    effective = scale(down_weight, block_scales.T)

    pg = pick(projector.reshape(4, 16, -1), x, 0)[None, None]
    got = swap(pg, "zq", 2)
    far, effective, *near = lax.optimization_barrier((far, effective, *near))
    got, *near = lax.optimization_barrier((got, *near))
    pg = placed(pg, got, zq >> 1, 0)
    pg = join(pg.reshape(2, 1, 16, -1), "zq", 1, zq & 1, 1).reshape(4, 1, 1, 16, -1)

    send, near = band(core, effective, near)
    near_got = swap(send, "co", 1)
    far, pg = lax.optimization_barrier((gather(far, "y").reshape(256, rows), pg))
    send, far = band(core, effective, [far])
    far_got = swap(send, "co", 1)

    pg = join(pg, "dp", 1, x & 1, 2)
    pg = join(pg, "dp", 2, x >> 1, 1).reshape(256, -1)

    column = jnp.arange(half)[None, :]
    place = (column == zp * 256 + zq * 64 + jnp.arange(64)[:, None]).astype(BF)
    res = jnp.dot(residual, place, preferred_element_type=F32).astype(BF).reshape(8, 64, half)
    blocks = lambda v: v.reshape(4, 64, half)
    acc = combine(jnp.stack([y, zh]), blocks(near), blocks(near_got), blocks(far), blocks(far_got), res)
    hid = exchange(acc.reshape(8, BLOCK, 256), ("zq", "zp"))
    hid = jnp.sum(hid.astype(F32), 0).astype(BF)

    mine = (jnp.arange(BLOCK) // 4 == zp * 16 + core * 8 + y * 2 + zh)[:, None]
    own_student = jnp.where(mine, jnp.tile(student.astype(F32), (32, 1)), 0.0)
    err = jnp.dot(hid, pg, preferred_element_type=F32) - own_student
    err = jnp.sum(exchange(err.astype(BF).reshape(16, 8, -1), ("zp", "co", "y")).astype(F32), 0)
    hid_two = after(jnp.stack([hid, swap(hid, "dp", 1)]), err)
    hid_all = jnp.concatenate([hid_two, swap(hid_two, "dp", 2)])
    hid_all = jnp.take(hid_all, x ^ jnp.arange(4), axis=0).reshape(512, 256)
    err = err + swap(err.astype(BF), "zh", 1).astype(F32)
    err, hid_all = lax.optimization_barrier((err, hid_all))

    passage = segments[0]
    same = (passage[:, None] == passage[None, :]).astype(F32)
    weight_all = F32(512) / (COUNT * jnp.sum(same, axis=1))
    weight = lax.dynamic_slice_in_dim(weight_all, zq * 128 + zp * 64 + core * 32 + y * 8, 8, 0)
    scaled_f = weight[:, None] * err
    student_grad = -lax.dynamic_slice_in_dim(scaled_f, zh * 4, 4, 0)
    scaled = lax.all_gather(scaled_f.astype(BF), "co")

    quarters = jnp.moveaxis(scaled.reshape(2, 8, 4, 384), 2, 0)[:, None]
    quarters = jnp.broadcast_to(quarters, (4, 8, 2, 8, 384)).reshape(32, 2, 8, 384)
    scaled_all = exchange(quarters, ("dp", "zp", "y")).reshape(8, 4, 2, 8, 384)
    scaled_all = jnp.swapaxes(scaled_all, 1, 2).reshape(512, 384)
    grad = lax.dot_general(hid_all, scaled_all, (((0,), (0,)), ((), ())), preferred_element_type=F32)
    grad = jnp.sum(exchange(grad.astype(BF).reshape(4, 64, 384), "zq").astype(F32), 0).astype(BF)
    pieces = gather(grad, "dp").reshape(4, 64, 384)
    total = jnp.concatenate([pieces[i] for i in range(4)], 1)
    factor = 1.0 / math.sqrt(512 * lax.axis_size("dp"))
    return (student_grad, total.astype(F32) * factor)


def solution(mesh):
    names = ("dp", "zq", "zp", "co", "y", "zh")
    fine = Mesh(mesh.devices.reshape(4, 4, 2, 2, 4, 2), names)
    trow, tcol = names[1:4], names[4:]
    in_specs = (
        P(("dp",) + tcol, trow),
        P(trow, tcol),
        P(trow, tcol),
        P("dp", tcol + trow),
        P(tcol + trow, None),
        P(("dp",) + trow + tcol, None),
        P("dp", None),
    )
    out_specs = (P(("dp",) + trow + tcol, None), P(tcol + trow, None))
    return jax.shard_map(shards, mesh=fine, in_specs=in_specs, out_specs=out_specs, check_vma=False)
```
